256 devices in a mesh: section: 64 (over x_lo, y, z), team: 4 (over x_hi, core).
Axes of the slice: x: 4 (x_hi: 2, x_lo: 2; x = x_hi * 2 + x_lo), y: 4, z: 8, core: 2. Of those that a mesh axis runs over, the one named last changes fastest.
Arguments:
- features: bfloat16 [65536, 128], P(('section', 'team')), may hold values from -6 to 6
- weight: bfloat16 [128, 256], replicated, may hold values from -0.5 to 0.5
- tiles: bfloat16 [64, 4, 256, 128, 128], P('section', 'team'), may hold values from -0.4375 to 0.4375
- tile_rows: int32 [64, 4, 256], P('section', 'team'), may hold values from 0 to 7, as said below
- tile_cols: int32 [64, 4, 256], P('section', 'team'), may hold values from 0 to 127, as said below
- tile_count: int32 [64, 4], P('section', 'team'), may hold values from 1 to 256, as said below
- cotangent: bfloat16 [65536, 256], P(('section', 'team')), may hold values from -6 to 6
Outputs:
- output: bfloat16 [65536, 256], P(('section', 'team'))
- grad_features: bfloat16 [65536, 128], P(('section', 'team'))
- grad_weight: float32 [128, 256], replicated
The draws below stay inside these ranges and needn't reach their ends.
Inputs may be any that keep to these rules, and one draw needn't show every extreme that they name: `tile_rows`: row tile of a slot, from 0 to 7. `tile_cols`: column tile of a slot, from 0 to 127; some column tiles are named far more often than others. The live slots of a device are its first tile_count slots; some device has all 256 live.
All inputs are finite; a program needn't handle non-finite values.
Results may differ from the reference program's by a relative error of at most 0.02.
Values may be sent and summed in bfloat16 or wider, within the bound.
No kernel may reach another device: no remote copies, remote signals or barrier semaphores. Data moves between devices by JAX's collectives and lax.ppermute only.
A program may use at most 128 MiB of HBM per device.

```python
import jax
import jax.numpy as jnp
from jax import lax

FIN = 128
FOUT = 256
TILE = 128
TILES = 256
SECTIONS = 64
TEAMS = 4
KT = 2
RS = 8
CT = 128
NODES = 65536


def draw_tile_rows(key, part):
    key = jax.random.fold_in(key, 11)
    return jax.random.randint(key, (SECTIONS, TEAMS, TILES), 0, RS).astype(jnp.int32)


def draw_tile_cols(key, part):
    key = jax.random.fold_in(key, 12)
    first, second, third, fourth = jax.random.split(key, 4)
    shape = (SECTIONS, TEAMS, TILES)
    one = jax.random.randint(first, shape, 0, CT)
    two = jax.random.randint(second, shape, 0, CT)
    three = jax.random.randint(third, shape, 0, CT)
    lowest = jnp.minimum(jnp.minimum(one, two), three)
    order = jax.random.permutation(fourth, CT)
    return order[lowest].astype(jnp.int32)


def draw_tile_count(key, part):
    key = jax.random.fold_in(key, 13)
    first, second = jax.random.split(key)
    lowest = max(1, TILES // 8)
    level = jax.random.randint(first, (SECTIONS * TEAMS,), 0, 64)
    count = lowest + (TILES - lowest) * level * level // 3969
    place = jax.random.randint(second, (), 0, SECTIONS * TEAMS)
    count = count.at[place].set(TILES)
    return count.reshape(SECTIONS, TEAMS).astype(jnp.int32)


def steps_of(key, extent, shards, least, largest):
    def one(axis_at, parts):
        steps = jax.random.uniform(jax.random.fold_in(jax.random.fold_in(key, 6), axis_at), (parts,), jnp.float32, least / len(shards), largest / len(shards))
        return jnp.repeat(jnp.exp(steps), extent[axis_at] // parts).reshape((-1,) + (1,) * (len(extent) - axis_at - 1))

    loudness = one(*shards[0])
    for cut in shards[1:]:
        loudness = loudness * one(*cut)
    return loudness


def centred(rng, shape, scale, limit, pieces=(), kind=jnp.bfloat16):
    drawn = scale * jax.random.normal(rng, shape, jnp.float32)
    if pieces:
        drawn = drawn * steps_of(rng, shape, pieces, -0.22, 0.18)
    return jnp.clip(drawn, -limit, limit).astype(kind)


def setup_inputs(seed: int = 0) -> dict:
    streams_of = jax.random.split(jax.random.key(seed), 8)
    return {
        "features": centred(streams_of[0], (NODES, FIN), 1.0, 6.0, ((0, 256),)),
        "weight": centred(streams_of[1], (FIN, FOUT), FIN ** -0.5, 0.5),
        "tiles": centred(streams_of[2], (SECTIONS, TEAMS, TILES, TILE, TILE), 0.03, 0.4375, ((0, 64), (1, 4))),
        "tile_rows": draw_tile_rows(jax.random.fold_in(streams_of[7], 71), 0),
        "tile_cols": draw_tile_cols(jax.random.fold_in(streams_of[7], 71), 0),
        "tile_count": draw_tile_count(jax.random.fold_in(streams_of[7], 71), 0),
        "cotangent": centred(streams_of[6], (NODES, FOUT), 1.0, 6.0, ((0, 256),)),
    }


def reference(features, weight, tiles, tile_rows, tile_cols, tile_count, cotangent):
    feats = features.reshape(SECTIONS, TEAMS, KT, TILE, FIN)
    slot_ids = jnp.arange(TILES, dtype=jnp.int32)

    def member_blocks(member):
        return feats[:, member].reshape(CT, TILE, FIN).astype(jnp.float32)

    def section_forward(section_id):
        total = jnp.zeros((RS, TILE, FIN), jnp.float32)
        for member in range(TEAMS):
            live = (slot_ids < tile_count[section_id, member]).astype(jnp.float32)
            picked = member_blocks(member)[tile_cols[section_id, member]]
            prod = jnp.einsum('sij,sjf->sif', tiles[section_id, member].astype(jnp.float32), picked)
            prod = prod * live[:, None, None]
            total = total + jax.ops.segment_sum(prod, tile_rows[section_id, member], num_segments=RS)
        return total.reshape(RS * TILE, FIN)

    aggregated = lax.map(section_forward, jnp.arange(SECTIONS, dtype=jnp.int32)).reshape(NODES, FIN).astype(jnp.bfloat16)
    pre = jnp.dot(aggregated, weight, preferred_element_type=jnp.float32)
    sig = jax.nn.sigmoid(pre)
    output = (pre * sig).astype(jnp.bfloat16)
    grad_pre = (cotangent.astype(jnp.float32) * sig * (1.0 + pre * (1.0 - sig))).astype(jnp.bfloat16)
    grad_weight = jnp.dot(aggregated.T, grad_pre, preferred_element_type=jnp.float32) * (NODES ** -0.5)
    back = jnp.dot(grad_pre, weight.T, preferred_element_type=jnp.float32).astype(jnp.bfloat16)
    backs = back.reshape(SECTIONS, RS, TILE, FIN)

    def section_backward(carry, section_id):
        fresh = []
        for member in range(TEAMS):
            live = (slot_ids < tile_count[section_id, member]).astype(jnp.float32)
            picked = backs[section_id][tile_rows[section_id, member]].astype(jnp.float32)
            prod = jnp.einsum('sij,sif->sjf', tiles[section_id, member].astype(jnp.float32), picked)
            prod = prod * live[:, None, None]
            fresh.append(carry[member] + jax.ops.segment_sum(prod, tile_cols[section_id, member], num_segments=CT))
        return jnp.stack(fresh), None

    start = jnp.zeros((TEAMS, CT, TILE, FIN), jnp.float32)
    carry, unused = lax.scan(section_backward, start, jnp.arange(SECTIONS, dtype=jnp.int32))
    grad_features = carry.reshape(TEAMS, SECTIONS, KT, TILE, FIN).transpose(1, 0, 2, 3, 4).reshape(NODES, FIN).astype(jnp.bfloat16)
    return (output, grad_features, grad_weight)
```

```python
import math

import jax
import jax.numpy as jnp
from jax import lax
from jax.experimental import pallas as pl
from jax.experimental.pallas import tpu as pltpu
from jax.sharding import PartitionSpec as P

NX, NY, NZ = 2, 4, 8
CHUNKS = 8
STEP = 4
F32 = jnp.float32
BF16 = jnp.bfloat16


def section_index(x, y, z):
    return ((x % NX) * NY + y % NY) * NZ + z % NZ


def send(value, dx=0, dy=0, dz=0):
    pairs = [
        (section_index(x, y, z), section_index(x + dx, y + dy, z + dz))
        for x in range(NX)
        for y in range(NY)
        for z in range(NZ)
    ]
    return lax.ppermute(value, "section", pairs)


def send_section_xor(value, mask):
    return lax.ppermute(value, "section", [(s, s ^ mask) for s in range(NX * NY * NZ)])


def send_team(value, mask):
    return lax.ppermute(value, "team", [(t, t ^ mask) for t in range(4)])


def start_tiles(tiles, tbuf, tsem, count, per):
    for c in range(CHUNKS):

        @pl.when(c * per < count)
        def _():
            part = pl.ds(c * per, per)
            pltpu.make_async_copy(tiles.at[part], tbuf.at[part], tsem.at[c]).start()


def over_tiles(tiles, tbuf, tsem, count, per, step_fn):
    for c in range(CHUNKS):

        @pl.when(c * per < count)
        def _():
            part = pl.ds(c * per, per)
            pltpu.make_async_copy(tiles.at[part], tbuf.at[part], tsem.at[c]).wait()
            left = jnp.minimum(count - c * per, per)

            def body(i, carry):
                step_fn(c * per + i * STEP)
                return carry

            lax.fori_loop(0, (left + STEP - 1) // STEP, body, 0)


def forward_kernel(spans, per, rows, cols, count_ref, tiles, *refs):
    n = len(spans)
    pieces = refs[:n]
    out, feat, tbuf, acc, tsem, fsem = refs[n:]
    count = count_ref[0]
    copies = []
    for i, (at, size) in enumerate(spans):
        copies.append(pltpu.make_async_copy(pieces[i], feat.at[pl.ds(at, size)], fsem.at[i]))
        copies[-1].start()
    start_tiles(tiles, tbuf, tsem, count, per)
    acc[...] = jnp.zeros_like(acc)
    for copy in copies:
        copy.wait()

    def step(s):
        prods = [
            jnp.dot(tbuf[s + j], feat[cols[s + j]], preferred_element_type=F32)
            for j in range(STEP)
        ]
        for j in range(STEP):
            r = rows[s + j]
            acc[r] = acc[r] + prods[j]

    over_tiles(tiles, tbuf, tsem, count, per, step)
    out[...] = acc[: out.shape[0]].astype(out.dtype)


def forward_call(rows, cols, count, tiles, pieces, spans, row_tiles):
    slots, tile, _ = tiles.shape
    fin = pieces[0].shape[-1]
    col_tiles = sum(size for _, size in spans)
    smem = pl.BlockSpec(memory_space=pltpu.SMEM)
    hbm = pl.BlockSpec(memory_space=pl.ANY)
    per = slots // CHUNKS

    def kernel(*refs):
        forward_kernel(spans, per, *refs)

    return pl.pallas_call(
        kernel,
        out_shape=jax.ShapeDtypeStruct((row_tiles, tile, fin), BF16),
        in_specs=[smem] * 3 + [hbm] * (1 + len(pieces)),
        out_specs=pl.BlockSpec(memory_space=pltpu.VMEM),
        scratch_shapes=[
            pltpu.VMEM((col_tiles, tile, fin), BF16),
            pltpu.VMEM((slots, tile, tile), BF16),
            pltpu.VMEM((row_tiles + 1, tile, fin), F32),
            pltpu.SemaphoreType.DMA((CHUNKS,)),
            pltpu.SemaphoreType.DMA((len(pieces),)),
        ],
        compiler_params=pltpu.CompilerParams(vmem_limit_bytes=40 * 2**20),
        name="tiles_forward",
    )(rows, cols, count, tiles, *pieces)


def backward_kernel(
    per, half, rows, cols, count_ref, member_ref, tiles, sum_a, sum_b, c0, c1, c2, c3, weight,
    out, wpart, *refs,
):
    n = len(half)
    outs = refs[:n]
    tbuf, acc, agg, gpre, backs, wfull, tsem = refs[n:]
    count = count_ref[0]
    member = member_ref[0]
    start_tiles(tiles, tbuf, tsem, count, per)
    row_tiles, tile, fin = sum_a.shape
    node_dev = out.shape[0]
    per_dev = node_dev // tile
    total = sum_a[...].astype(F32) + sum_b[...].astype(F32)
    agg[...] = total.astype(BF16).reshape(agg.shape)
    for d, cot in enumerate((c0, c1, c2, c3)):
        who = member ^ d
        at = pl.multiple_of(who * node_dev, node_dev)
        mine = agg[pl.ds(at, node_dev), :]
        pre = jnp.dot(mine, weight[...], preferred_element_type=F32)
        sig = jax.nn.sigmoid(pre)
        if d == 0:
            out[...] = (pre * sig).astype(BF16)
        grad = (cot[...].astype(F32) * sig * (1.0 + pre * (1.0 - sig))).astype(BF16)
        gpre[pl.ds(at, node_dev), :] = grad
        back = lax.dot_general(
            weight[...], grad, (((1,), (1,)), ((), ())), preferred_element_type=F32
        ).astype(BF16)
        for j in range(per_dev):
            backs[who * per_dev + j] = back[:, j * tile : (j + 1) * tile]
    wfull[...] = lax.dot_general(
        agg[...], gpre[...], (((0,), (0,)), ((), ())), preferred_element_type=F32
    )
    share = wpart.shape[0]
    wpart[...] = wfull[pl.ds(pl.multiple_of(member * share, share), share), :]
    acc[...] = jnp.zeros_like(acc)

    def step(s):
        prods = [
            jnp.dot(backs[rows[s + j]], tbuf[s + j], preferred_element_type=F32)
            for j in range(STEP)
        ]
        for j in range(STEP):
            c = cols[s + j]
            acc[c] = acc[c] + prods[j]

    over_tiles(tiles, tbuf, tsem, count, per, step)
    for i, (at, size) in enumerate(half):
        outs[i][...] = acc[pl.ds(at, size)].astype(BF16)


def backward_call(rows, cols, count, member, tiles, sum_a, sum_b, cots, weight, spans):
    slots, tile, _ = tiles.shape
    row_tiles, _, fin = sum_a.shape
    node_dev, fout = cots[0].shape
    nodes = row_tiles * tile
    col_tiles = sum(size for _, size in spans)
    smem = pl.BlockSpec(memory_space=pltpu.SMEM)
    vmem = pl.BlockSpec(memory_space=pltpu.VMEM)
    hbm = pl.BlockSpec(memory_space=pl.ANY)
    per = slots // CHUNKS

    def kernel(*refs):
        backward_kernel(per, spans, *refs)

    return pl.pallas_call(
        kernel,
        out_shape=[
            jax.ShapeDtypeStruct((node_dev, fout), BF16),
            jax.ShapeDtypeStruct((fin // 4, fout), F32),
        ]
        + [jax.ShapeDtypeStruct((size, fin, tile), BF16) for _, size in spans],
        in_specs=[smem] * 4 + [hbm] + [vmem] * 7,
        out_specs=[vmem] * (2 + len(spans)),
        scratch_shapes=[
            pltpu.VMEM((slots, tile, tile), BF16),
            pltpu.VMEM((col_tiles + 1, fin, tile), F32),
            pltpu.VMEM((nodes, fin), BF16),
            pltpu.VMEM((nodes, fout), BF16),
            pltpu.VMEM((row_tiles, fin, tile), BF16),
            pltpu.VMEM((fin, fout), F32),
            pltpu.SemaphoreType.DMA((CHUNKS,)),
        ],
        compiler_params=pltpu.CompilerParams(vmem_limit_bytes=48 * 2**20),
        name="dense_and_tiles_backward",
    )(rows, cols, count, member, tiles, sum_a, sum_b, *cots, weight)


def add(*terms):
    total = terms[0].astype(F32)
    for term in terms[1:]:
        total = total + term.astype(F32)
    return total


def gather_features(features, tile):
    fin = features.shape[1]
    mine = features.reshape(-1, tile, fin)
    other = send(mine, dx=1)
    even = jnp.stack([mine[0], other[0]])
    odd = jnp.stack([mine[1], other[1]])

    plane = jnp.concatenate([even] + [send(even, dy=-d) for d in range(1, NY)])
    up, down = [plane], [plane]
    for _ in range(NZ // 2 - 1):
        up.append(send(up[-1], dz=-1))
        down.append(send(down[-1], dz=1))
    half = plane.shape[0] // 2
    far_up = send(up[-1][:half], dz=-1)
    far_down = send(down[-1][half:], dz=1)
    size = plane.shape[0]
    pieces = [plane, *up[1:], far_up, far_down, *down[:0:-1]]
    spans = [(i * size, size) for i in range(NZ // 2)]
    spans += [(NZ // 2 * size, half), (NZ // 2 * size + half, half)]
    spans += [(i * size, size) for i in range(NZ // 2 + 1, NZ)]

    line = jnp.concatenate([odd] + [send(odd, dz=-d) for d in range(1, NZ)])
    size2 = line.shape[0]
    next_up = send(line, dy=-1)
    next_down = send(line, dy=1)
    half2 = size2 // 2
    far2_up = send(next_up[:half2], dy=-1)
    far2_down = send(next_down[half2:], dy=1)
    base = NZ * size
    pieces += [line, next_up, far2_up, far2_down, next_down]
    spans += [
        (base, size2),
        (base + size2, size2),
        (base + 2 * size2, half2),
        (base + 2 * size2 + half2, half2),
        (base + 3 * size2, size2),
    ]
    return pieces, spans


def relative_columns(cols, me):
    owner = cols // 2
    odd = cols % 2
    dx = (owner // (NY * NZ)) ^ (me // (NY * NZ))
    dy = (owner // NZ - me // NZ) % NY
    dz = (owner - me) % NZ
    even_at = (dz * NY + dy) * NX + dx
    odd_at = NX * NY * NZ + (dy * NZ + dz) * NX + dx
    return jnp.where(odd == 1, odd_at, even_at)


def scatter_sum(parts):
    g0, g1, g2, g3, g4a, g4b, g5, g6, g7, h0, h1, h2a, h2b, h3 = parts
    half = g4a.shape[0]
    r = send(g4a, dz=1)
    u = jnp.concatenate([add(g3[:half], r).astype(BF16), g3[half:]])
    r = send(u, dz=1)
    u = add(g2, r).astype(BF16)
    r = send(u, dz=1)
    u = add(g1, r).astype(BF16)
    from_up = send(u, dz=1)
    r = send(g4b, dz=-1)
    u = jnp.concatenate([g5[:half], add(g5[half:], r).astype(BF16)])
    r = send(u, dz=-1)
    u = add(g6, r).astype(BF16)
    r = send(u, dz=-1)
    u = add(g7, r).astype(BF16)
    from_down = send(u, dz=-1)
    plane = add(g0, from_up, from_down)
    plane_b = plane.astype(BF16)
    even = add(plane[:NX], *[send(plane_b[NX * d : NX * d + NX], dy=d) for d in range(1, NY)])

    half2 = h2a.shape[0]
    r1 = send(h2a, dy=1)
    r3 = send(h2b, dy=-1)
    u1 = jnp.concatenate([add(h1[:half2], r1).astype(BF16), h1[half2:]])
    u3 = jnp.concatenate([h3[:half2], add(h3[half2:], r3).astype(BF16)])
    line = add(h0, send(u1, dy=1), send(u3, dy=-1))
    line_b = line.astype(BF16)
    odd = add(line[:NX], *[send(line_b[NX * d : NX * d + NX], dz=d) for d in range(1, NZ)])

    both = jnp.stack([even, odd], axis=1)
    return both[0] + send(both[1].astype(BF16), dx=1).astype(F32)


def reduce_weight(part, scale):
    total = part
    for mask in (1, 2, 4, 8, 16, 32):
        total = total + send_section_xor(total, mask)
    member = lax.axis_index("team")
    other = send_team(total, 1)
    low = member % 2 == 0
    pair = jnp.where(low, jnp.concatenate([total, other]), jnp.concatenate([other, total]))
    other = send_team(pair, 2)
    low = member // 2 == 0
    whole = jnp.where(low, jnp.concatenate([pair, other]), jnp.concatenate([other, pair]))
    return whole * scale


def per_device(features, weight, tiles, tile_rows, tile_cols, tile_count, cotangent):
    node_dev, fin = features.shape
    tile = tiles.shape[-1]
    slots = tiles.shape[2]
    sections = lax.axis_size("section")
    teams = lax.axis_size("team")
    per_dev = node_dev // tile
    row_tiles = per_dev * teams
    col_tiles = per_dev * sections
    scale = 1.0 / math.sqrt(node_dev * sections * teams)
    slab = tiles.reshape(slots, tile, tile)
    count = tile_count.reshape(1)
    live = jnp.arange(slots, dtype=jnp.int32) < count
    rows = tile_rows.reshape(slots)
    cols = relative_columns(tile_cols.reshape(slots), lax.axis_index("section"))
    rows_fwd = jnp.where(live, rows, row_tiles)
    cols_bwd = jnp.where(live, cols, col_tiles)
    member = lax.axis_index("team").astype(jnp.int32).reshape(1)

    pieces, spans = gather_features(features, tile)
    cot1 = send_team(cotangent, 1)
    both = send_team(jnp.stack([cotangent, cot1]), 2)
    cots = (cotangent, cot1, both[0], both[1])

    partial_sum = forward_call(rows_fwd, cols, count, slab, pieces, spans, row_tiles)
    pair = add(partial_sum, send_team(partial_sum, 1)).astype(BF16)
    output, weight_part, *parts = backward_call(
        rows, cols_bwd, count, member, slab, pair, send_team(pair, 2), cots, weight, spans
    )
    grad_weight = reduce_weight(weight_part, scale)
    total = scatter_sum(parts)
    grad_features = total.transpose(0, 2, 1).reshape(node_dev, fin).astype(BF16)
    return output, grad_features, grad_weight


def solution(mesh):
    in_specs = (
        P(("section", "team"), None),
        P(),
        P("section", "team", None, None, None),
        P("section", "team", None),
        P("section", "team", None),
        P("section", "team"),
        P(("section", "team"), None),
    )
    out_specs = (P(("section", "team"), None), P(("section", "team"), None), P())
    return jax.shard_map(
        per_device, mesh=mesh, in_specs=in_specs, out_specs=out_specs, check_vma=False
    )
```

```python
import math

import jax
import jax.numpy as jnp
from jax import lax
from jax.experimental import pallas as pl
from jax.experimental.pallas import tpu as pltpu
from jax.sharding import PartitionSpec as P

NX, NY, NZ = 2, 4, 8
UNROLL = 16
NEAR = (0, 1, 2, 6, 7)
FAR = (3, 4, 5)
F32 = jnp.float32
BF16 = jnp.bfloat16
VMEM_LIMIT = 56 * 2**20


def section_index(x, y, z):
    return ((x % NX) * NY + y % NY) * NZ + z % NZ


def send(value, dx=0, dy=0, dz=0):
    pairs = [
        (section_index(x, y, z), section_index(x + dx, y + dy, z + dz))
        for x in range(NX)
        for y in range(NY)
        for z in range(NZ)
    ]
    return lax.ppermute(value, "section", pairs)


def send_team(value, mask):
    return lax.ppermute(value, "team", [(t, t ^ mask) for t in range(4)])


def fence(*arrays):
    return lax.optimization_barrier(arrays)


def add(*terms):
    total = terms[0].astype(F32)
    for term in terms[1:]:
        total = total + term.astype(F32)
    return total


def join(*arrays):
    return jnp.concatenate(arrays)


def sort_kernel(row_tiles, rows, cols, info, out):
    slots = rows.shape[0]
    region = slots + UNROLL
    length = 2 * region + UNROLL
    blocks = NY * NX * 2
    count, me = info[0], info[1]

    def put(p, slot, row, col):
        out[p] = slot
        out[length + p] = row
        out[2 * length + p] = col

    def body(step, carry):
        near_n, far_n = carry
        for j in range(8):
            i = step * 8 + j
            col = cols[i]
            owner = col >> 1
            dx = (owner >> 5) ^ (me >> 5)
            dy = ((owner >> 3) - (me >> 3)) & (NY - 1)
            dz = (owner - me) & (NZ - 1)
            far = ((dz >= FAR[0]) & (dz <= FAR[-1])).astype(jnp.int32)
            live = (i < count).astype(jnp.int32)
            plane = jnp.where(dz < FAR[0], dz, dz - FAR[0])
            place = plane * blocks + dy * (NX * 2) + dx * 2 + (col & 1)
            spot = jnp.where(far == 1, region + far_n, near_n)
            put(jnp.where(live == 1, spot, 2 * region), i, rows[i], place)
            near_n = near_n + live * (1 - far)
            far_n = far_n + live * far
        return near_n, far_n

    zero = jnp.int32(0)
    near_n, far_n = lax.fori_loop(0, slots // 8, body, (zero, zero))
    for j in range(UNROLL):
        put(near_n + j, 0, row_tiles, len(NEAR) * blocks)
        put(region + far_n + j, 0, row_tiles, len(FAR) * blocks)
    out[3 * length] = (near_n + UNROLL - 1) // UNROLL
    out[3 * length + 1] = (far_n + UNROLL - 1) // UNROLL


def sort_slots(rows, cols, count, me, row_tiles):
    smem = pl.BlockSpec(memory_space=pltpu.SMEM)
    length = 2 * (rows.shape[0] + UNROLL) + UNROLL

    def kernel(*refs):
        sort_kernel(row_tiles, *refs)

    return pl.pallas_call(
        kernel,
        out_shape=jax.ShapeDtypeStruct((3 * length + 2,), jnp.int32),
        in_specs=[smem] * 3,
        out_specs=smem,
        name="sort_slots",
    )(rows, cols, jnp.stack([count, me.astype(jnp.int32)]))


class Slots:
    def __init__(self, ref, group):
        self.ref = ref
        self.length = (ref.shape[0] - 2) // 3
        self.start = group * ((self.length - UNROLL) // 2)
        self.chunks = ref[3 * self.length + group]

    def get(self, field, i):
        return self.ref[field * self.length + self.start + i]

    def slot(self, i):
        return self.get(0, i)

    def row(self, i):
        return self.get(1, i)

    def col(self, i):
        return self.get(2, i)

    def fetch(self, tiles, buf, sem):
        def body(c, carry):
            for j in range(UNROLL):
                i = c * UNROLL + j
                pltpu.make_async_copy(tiles.at[self.slot(i)], buf.at[i], sem.at[c]).start()
            return carry

        lax.fori_loop(0, self.chunks, body, 0)

    def each(self, tiles, buf, sem, fn):
        def body(c, carry):
            part = pl.ds(c * UNROLL, UNROLL)
            pltpu.make_async_copy(tiles.at[pl.ds(0, UNROLL)], buf.at[part], sem.at[c]).wait()
            for j in range(UNROLL):
                fn(c * UNROLL + j)
            return carry

        lax.fori_loop(0, self.chunks, body, 0)


def forward_kernel(group, spans, slots_ref, tiles, *refs):
    n = len(spans)
    pieces = refs[:n]
    before = refs[n] if group else None
    out, feat, buf, acc, tsem, fsem = refs[n + group :]
    slots = Slots(slots_ref, group)
    copies = []
    for i, (at, size) in enumerate(spans):
        copies.append(pltpu.make_async_copy(pieces[i], feat.at[pl.ds(at, size)], fsem.at[i]))
        copies[-1].start()
    slots.fetch(tiles, buf, tsem)
    acc[...] = before[...] if group else jnp.zeros_like(acc)
    feat[feat.shape[0] - 1] = jnp.zeros(feat.shape[1:], feat.dtype)
    for copy in copies:
        copy.wait()

    def one(i):
        r = slots.row(i)
        acc[r] = acc[r] + jnp.dot(buf[i], feat[slots.col(i)], preferred_element_type=F32)

    slots.each(tiles, buf, tsem, one)
    out[...] = acc[: out.shape[0]].astype(out.dtype)


def forward_call(group, slot_info, tiles, pieces, spans, before, row_tiles):
    slots, tile, _ = tiles.shape
    fin = pieces[0].shape[-1]
    blocks = sum(size for _, size in spans)
    smem = pl.BlockSpec(memory_space=pltpu.SMEM)
    vmem = pl.BlockSpec(memory_space=pltpu.VMEM)
    hbm = pl.BlockSpec(memory_space=pl.ANY)

    def kernel(*refs):
        forward_kernel(group, spans, *refs)

    shape = (row_tiles, tile, fin) if group else (row_tiles + 1, tile, fin)
    return pl.pallas_call(
        kernel,
        out_shape=jax.ShapeDtypeStruct(shape, BF16 if group else F32),
        in_specs=[smem] + [hbm] * (1 + len(pieces)) + [vmem] * group,
        out_specs=vmem,
        scratch_shapes=[
            pltpu.VMEM((blocks + 1, tile, fin), BF16),
            pltpu.VMEM((slots, tile, tile), BF16),
            pltpu.VMEM((row_tiles + 1, tile, fin), F32),
            pltpu.SemaphoreType.DMA((slots // UNROLL,)),
            pltpu.SemaphoreType.DMA((len(pieces),)),
        ],
        compiler_params=pltpu.CompilerParams(vmem_limit_bytes=VMEM_LIMIT),
        cost_estimate=pl.CostEstimate(
            flops=blocks * 2 * 2 * tile**3, bytes_accessed=blocks * 4 * tile**2, transcendentals=0
        ),
        name="forward_far" if group else "forward_near",
    )(slot_info, tiles, *pieces, *([before] if group else []))


def backward_tiles(slots, layout, tiles, backs, outs, rider, none, buf, acc, stage, tsem, osem):
    def one(i):
        c = slots.col(i)
        acc[c] = acc[c] + jnp.dot(backs[slots.row(i)], buf[i], preferred_element_type=F32)

    slots.each(tiles, buf, tsem, one)
    copies = []
    size = acc.shape[0] // len(layout)
    for i, kind in enumerate(layout):
        part = pl.ds(i * size, size)
        stage[part] = acc[part].astype(BF16)
        copies.append(
            pltpu.make_async_copy(stage.at[part], outs[i].at[pl.ds(0, size)], osem.at[i, 0])
        )
        copies[-1].start()
        if kind:
            extra = rider if kind == "rider" else none
            copies.append(
                pltpu.make_async_copy(extra, outs[i].at[pl.ds(size, 1)], osem.at[i, 1])
            )
            copies[-1].start()
    for copy in copies:
        copy.wait()


def piece_shapes(layout, size, fin, tile):
    return [
        jax.ShapeDtypeStruct((size + 1 if kind else size, fin, tile), BF16) for kind in layout
    ]


def backward_far_kernel(
    layout, slots_ref, member_ref, tiles, sum_a, sum_b, c0, c1, c2, c3, weight,
    out, rider, backs, *refs,
):
    n = len(layout)
    outs = refs[:n]
    buf, acc, stage, agg, gpre, wfull, none, tsem, osem = refs[n:]
    member = member_ref[0]
    slots = Slots(slots_ref, 1)
    slots.fetch(tiles, buf, tsem)
    _, tile, _ = sum_a.shape
    node_dev = out.shape[0]
    per_dev = node_dev // tile
    total = sum_a[...].astype(F32) + sum_b[...].astype(F32)
    agg[...] = total.astype(BF16).reshape(agg.shape)
    acc[...] = jnp.zeros_like(acc)
    for d, cot in enumerate((c0, c1, c2, c3)):
        who = member ^ d
        at = pl.multiple_of(who * node_dev, node_dev)
        mine = agg[pl.ds(at, node_dev), :]
        pre = jnp.dot(mine, weight[...], preferred_element_type=F32)
        sig = jax.nn.sigmoid(pre)
        if d == 0:
            out[...] = (pre * sig).astype(BF16)
        grad = (cot[...].astype(F32) * sig * (1.0 + pre * (1.0 - sig))).astype(BF16)
        gpre[pl.ds(at, node_dev), :] = grad
        back = lax.dot_general(
            weight[...], grad, (((1,), (1,)), ((), ())), preferred_element_type=F32
        ).astype(BF16)
        for j in range(per_dev):
            backs[who * per_dev + j] = back[:, j * tile : (j + 1) * tile]
    backs[backs.shape[0] - 1] = jnp.zeros(backs.shape[1:], BF16)
    none[...] = jnp.zeros_like(none)
    wfull[...] = lax.dot_general(
        agg[...], gpre[...], (((0,), (0,)), ((), ())), preferred_element_type=F32
    )
    fin, fout = wfull.shape
    share = fin // 2
    part = wfull[pl.ds(pl.multiple_of(member % 2 * share, share), share), :].astype(BF16)
    rider[0, pl.ds(0, share), :] = part[:, : fout // 2]
    rider[0, pl.ds(share, share), :] = part[:, fout // 2 :]
    backward_tiles(
        slots, layout, tiles, backs, outs, rider, none, buf, acc, stage, tsem, osem
    )


def backward_far_call(slot_info, member, tiles, sum_a, sum_b, cots, weight, size):
    slots, tile, _ = tiles.shape
    row_tiles, _, fin = sum_a.shape
    node_dev, fout = cots[0].shape
    nodes = row_tiles * tile
    layout = (None, "rider", None, "rider", None, "none")
    blocks = size * len(layout)
    smem = pl.BlockSpec(memory_space=pltpu.SMEM)
    vmem = pl.BlockSpec(memory_space=pltpu.VMEM)
    hbm = pl.BlockSpec(memory_space=pl.ANY)

    def kernel(*refs):
        backward_far_kernel(layout, *refs)

    return pl.pallas_call(
        kernel,
        out_shape=[
            jax.ShapeDtypeStruct((node_dev, fout), BF16),
            jax.ShapeDtypeStruct((1, fin, tile), BF16),
            jax.ShapeDtypeStruct((row_tiles + 1, fin, tile), BF16),
            *piece_shapes(layout, size, fin, tile),
        ],
        in_specs=[smem] * 2 + [hbm] + [vmem] * 7,
        out_specs=[vmem] * 3 + [hbm] * len(layout),
        scratch_shapes=[
            pltpu.VMEM((slots, tile, tile), BF16),
            pltpu.VMEM((blocks + 1, fin, tile), F32),
            pltpu.VMEM((blocks, fin, tile), BF16),
            pltpu.VMEM((nodes, fin), BF16),
            pltpu.VMEM((nodes, fout), BF16),
            pltpu.VMEM((fin, fout), F32),
            pltpu.VMEM((1, fin, tile), BF16),
            pltpu.SemaphoreType.DMA((slots // UNROLL,)),
            pltpu.SemaphoreType.DMA((len(layout), 2)),
        ],
        compiler_params=pltpu.CompilerParams(vmem_limit_bytes=VMEM_LIMIT),
        cost_estimate=pl.CostEstimate(
            flops=blocks * 2 * 2 * tile**3, bytes_accessed=blocks * 6 * tile**2, transcendentals=0
        ),
        name="dense_and_backward_far",
    )(slot_info, member, tiles, sum_a, sum_b, *cots, weight)


def backward_near_kernel(layout, slots_ref, tiles, backs, *refs):
    n = len(layout)
    outs = refs[:n]
    buf, acc, stage, none, tsem, osem = refs[n:]
    slots = Slots(slots_ref, 0)
    slots.fetch(tiles, buf, tsem)
    acc[...] = jnp.zeros_like(acc)
    none[...] = jnp.zeros_like(none)
    backward_tiles(slots, layout, tiles, backs, outs, None, none, buf, acc, stage, tsem, osem)


def backward_near_call(slot_info, tiles, backs, size):
    slots, tile, _ = tiles.shape
    fin = backs.shape[1]
    layout = (None, None) + (None, "none") * 4
    blocks = size * len(layout)
    smem = pl.BlockSpec(memory_space=pltpu.SMEM)
    vmem = pl.BlockSpec(memory_space=pltpu.VMEM)
    hbm = pl.BlockSpec(memory_space=pl.ANY)

    def kernel(*refs):
        backward_near_kernel(layout, *refs)

    return pl.pallas_call(
        kernel,
        out_shape=piece_shapes(layout, size, fin, tile),
        in_specs=[smem, hbm, vmem],
        out_specs=[hbm] * len(layout),
        scratch_shapes=[
            pltpu.VMEM((slots, tile, tile), BF16),
            pltpu.VMEM((blocks + 1, fin, tile), F32),
            pltpu.VMEM((blocks, fin, tile), BF16),
            pltpu.VMEM((1, fin, tile), BF16),
            pltpu.SemaphoreType.DMA((slots // UNROLL,)),
            pltpu.SemaphoreType.DMA((len(layout), 2)),
        ],
        compiler_params=pltpu.CompilerParams(vmem_limit_bytes=VMEM_LIMIT),
        cost_estimate=pl.CostEstimate(
            flops=blocks * 2 * 2 * tile**3, bytes_accessed=blocks * 6 * tile**2, transcendentals=0
        ),
        name="backward_near",
    )(slot_info, tiles, backs)


def gather_features(features, cotangent, tile):
    fin = features.shape[1]
    mine = features.reshape(-1, tile, fin)
    own = join(mine, send(mine, dx=1))
    cot1 = send_team(cotangent, 1)
    y1 = send(own, dy=-1)
    y3 = send(own, dy=1)
    y2 = send(own, dy=-2)
    up0, up1 = [join(own, y1)], [join(y2, y3)]
    down0, down1 = [up0[0]], [up1[0]]
    for step in range(4):
        up0.append(send(up0[-1], dz=-1))
        down1.append(send(down1[-1], dz=1))
        if step < 3:
            down0.append(send(down0[-1], dz=1))
            up1.append(send(up1[-1], dz=-1))
    cot2 = send_team(cotangent, 2)
    cot3 = send_team(cot1, 2)
    near = [up0[0], up1[0], up0[1], up1[1], up0[2], up1[2]]
    near += [down0[2], down1[2], down0[1], down1[1]]
    far = [up0[3], up1[3], up0[4], down1[4], down0[3], down1[3]]
    return near, far, (cotangent, cot1, cot2, cot3)


def spans_of(pieces):
    spans, at = [], 0
    for piece in pieces:
        spans.append((at, piece.shape[0]))
        at += piece.shape[0]
    return spans


def ring_sum(terms, dz):
    arrived = [send(terms[0], dz=dz)]
    for term in terms[1:]:
        arrived.append(send(add(term, arrived[-1]).astype(BF16), dz=dz))
    return arrived


def scatter_sums(near, far, rider):
    g0, g1, g2, g6, g7 = [near[2 * i : 2 * i + 2] for i in range(5)]
    g3, g4, g5 = [far[2 * i : 2 * i + 2] for i in range(3)]
    up0 = ring_sum((g4[0], g3[0], g2[0], g1[0]), 1)
    down1 = ring_sum((g4[1], g5[1], g6[1], g7[1]), -1)
    up1 = ring_sum((g3[1], g2[1], g1[1]), 1)
    down0 = ring_sum((g5[0], g6[0], g7[0]), -1)
    size = g0[0].shape[0]
    plane0 = add(g0[0], up0[-1], down0[-1])
    plane1 = add(g0[1], up1[-1][:size], down1[-1][:size]).astype(BF16)
    u1, u2, u3 = [part[size:] for part in up1]
    d1, d2, d3, d4 = [part[size:] for part in down1]
    rider = ((add(rider, d4) + add(u2, d2)) + (add(u1, d3) + add(u3, d1))).astype(BF16)
    half = size // 2
    got1 = send(join(plane0[half:].astype(BF16), rider), dy=1)
    got2 = send(join(plane1[:half], rider), dy=2)
    got3 = send(join(plane1[half:], rider), dy=-1)
    line = add(plane0[:half], got1[:half], got2[:half], got3[:half])
    rider = (add(rider, got2[half:]) + add(got1[half:], got3[half:])).astype(BF16)
    size = half
    half = size // 2
    got = send(join(line[half:].astype(BF16), rider), dx=1)
    total = add(line[:half], got[:half])
    weight = add(rider, got[half:])[0]
    share = weight.shape[0] // 2
    weight = jnp.concatenate([weight[:share], weight[share:]], axis=1)
    other = send_team(weight, 1)
    low = lax.axis_index("team") % 2 == 0
    return total, jnp.where(low, join(weight, other), join(other, weight))


def per_device(features, weight, tiles, tile_rows, tile_cols, tile_count, cotangent):
    node_dev, fin = features.shape
    tile = tiles.shape[-1]
    slots = tiles.shape[2]
    sections = lax.axis_size("section")
    teams = lax.axis_size("team")
    row_tiles = node_dev // tile * teams
    scale = 1.0 / math.sqrt(node_dev * sections * teams)
    slab = tiles.reshape(slots, tile, tile)
    slot_info = sort_slots(
        tile_rows.reshape(slots),
        tile_cols.reshape(slots),
        tile_count.reshape(()),
        lax.axis_index("section"),
        row_tiles,
    )
    member = lax.axis_index("team").astype(jnp.int32).reshape(1)

    near, far, cots = gather_features(features, cotangent, tile)
    partial_sum = forward_call(0, slot_info, slab, near, spans_of(near), None, row_tiles)
    partial_sum, *cots = fence(partial_sum, *cots)
    partial_sum = forward_call(1, slot_info, slab, far, spans_of(far), partial_sum, row_tiles)
    pair = add(partial_sum, send_team(partial_sum, 1)).astype(BF16)
    size = near[0].shape[0]
    output, rider, backs, *far_terms = backward_far_call(
        slot_info, member, slab, pair, send_team(pair, 2), cots, weight, size
    )
    near_terms = backward_near_call(slot_info, slab, backs, size)
    total, weight_sum = scatter_sums(near_terms, far_terms, rider)
    grad_features = total.transpose(0, 2, 1).reshape(node_dev, fin).astype(BF16)
    return output, grad_features, weight_sum * scale


def solution(mesh):
    in_specs = (
        P(("section", "team"), None),
        P(),
        P("section", "team", None, None, None),
        P("section", "team", None),
        P("section", "team", None),
        P("section", "team"),
        P(("section", "team"), None),
    )
    out_specs = (P(("section", "team"), None), P(("section", "team"), None), P())
    return jax.shard_map(
        per_device, mesh=mesh, in_specs=in_specs, out_specs=out_specs, check_vma=False
    )
```

```python
import math

import jax
import jax.numpy as jnp
from jax import lax
from jax.experimental import pallas as pl
from jax.experimental.pallas import tpu as pltpu
from jax.sharding import PartitionSpec as P

NX, NY, NZ = 2, 4, 8
UNROLL = 16
NEAR = (0, 1, 2, 6, 7)
FAR = (3, 4, 5)
F32 = jnp.float32
BF16 = jnp.bfloat16
VMEM_LIMIT = 24 * 2**20


def section_index(x, y, z):
    return ((x % NX) * NY + y % NY) * NZ + z % NZ


def send(value, dx=0, dy=0, dz=0):
    pairs = [
        (section_index(x, y, z), section_index(x + dx, y + dy, z + dz))
        for x in range(NX)
        for y in range(NY)
        for z in range(NZ)
    ]
    return lax.ppermute(value, "section", pairs)


def send_team(value, mask):
    return lax.ppermute(value, "team", [(t, t ^ mask) for t in range(4)])


def fence(*arrays):
    return lax.optimization_barrier(arrays)


def add(*terms):
    total = terms[0].astype(F32)
    for term in terms[1:]:
        total = total + term.astype(F32)
    return total


def join(*arrays):
    return jnp.concatenate(arrays)


def sort_kernel(row_tiles, keys, out):
    slots = keys.shape[0]
    region = slots + UNROLL
    blocks = NY * NX * 2

    def body(step, carry):
        near_n, far_n = carry
        for j in range(8):
            key = keys[step * 8 + j]
            is_near = (key >> 24) & 1
            is_far = key >> 25
            spot = jnp.where(is_far == 1, region + far_n, near_n)
            out[jnp.where(is_near + is_far == 1, spot, 2 * region)] = key
            near_n = near_n + is_near
            far_n = far_n + is_far
        return near_n, far_n

    zero = jnp.int32(0)
    near_n, far_n = lax.fori_loop(0, slots // 8, body, (zero, zero))
    for j in range(UNROLL):
        out[near_n + j] = (row_tiles << 8) + (len(NEAR) * blocks << 12)
        out[region + far_n + j] = (row_tiles << 8) + (len(FAR) * blocks << 12)
    out[2 * region + UNROLL] = (near_n + UNROLL - 1) // UNROLL
    out[2 * region + UNROLL + 1] = (far_n + UNROLL - 1) // UNROLL


def sort_slots(rows, cols, count, me, row_tiles):
    slots = rows.shape[0]
    blocks = NY * NX * 2
    owner = cols // 2
    dx = (owner // (NY * NZ)) ^ (me // (NY * NZ))
    dy = (owner // NZ - me // NZ) % NY
    dz = (owner - me) % NZ
    far = (dz >= FAR[0]) & (dz <= FAR[-1])
    place = jnp.where(dz < FAR[0], dz, dz - FAR[0]) * blocks + dy * (NX * 2) + dx * 2 + cols % 2
    ids = jnp.arange(slots, dtype=jnp.int32)
    group = jnp.where(ids < count, jnp.where(far, 2, 1), 0)
    keys = ids + (rows << 8) + (place << 12) + (group << 24)
    smem = pl.BlockSpec(memory_space=pltpu.SMEM)

    def kernel(*refs):
        sort_kernel(row_tiles, *refs)

    return pl.pallas_call(
        kernel,
        out_shape=jax.ShapeDtypeStruct((2 * (slots + UNROLL) + UNROLL + 2,), jnp.int32),
        in_specs=[smem],
        out_specs=smem,
        name="sort_slots",
    )(keys.astype(jnp.int32))


class Slots:
    def __init__(self, ref, group):
        self.ref = ref
        length = ref.shape[0] - 2
        self.start = group * ((length - UNROLL) // 2)
        self.chunks = ref[length + group]

    def slot(self, i):
        return self.ref[self.start + i] & 255

    def row(self, i):
        return (self.ref[self.start + i] >> 8) & 15

    def col(self, i):
        return (self.ref[self.start + i] >> 12) & 255

    def each(self, fn):
        def body(c, carry):
            for j in range(UNROLL):
                fn(c * UNROLL + j)
            return carry

        lax.fori_loop(0, self.chunks, body, 0)


def forward_kernel(group, spans, slots_ref, member_ref, tiles, *refs):
    n = len(spans)
    pieces = refs[:n]
    before = refs[n] if group else None
    *outs, feat, acc, fsem = refs[n + group :]
    slots = Slots(slots_ref, group)
    copies = []
    for i, (at, size) in enumerate(spans):
        copies.append(pltpu.make_async_copy(pieces[i], feat.at[pl.ds(at, size)], fsem.at[i]))
        copies[-1].start()
    acc[...] = before[...] if group else jnp.zeros_like(acc)
    feat[feat.shape[0] - 1] = jnp.zeros(feat.shape[1:], feat.dtype)
    for copy in copies:
        copy.wait()

    def one(i):
        r = slots.row(i)
        tile = tiles[slots.slot(i)]
        acc[r] = acc[r] + jnp.dot(tile, feat[slots.col(i)], preferred_element_type=F32)

    slots.each(one)
    if group:
        half = outs[0].shape[0]
        core = member_ref[0] % 2
        outs[0][...] = acc[pl.ds(core * half, half)].astype(BF16)
        outs[1][...] = acc[pl.ds((1 - core) * half, half)].astype(BF16)
    else:
        outs[0][...] = acc[...]


def forward_call(group, slot_info, member, tiles, pieces, spans, before, row_tiles):
    tile = tiles.shape[-1]
    fin = pieces[0].shape[-1]
    blocks = sum(size for _, size in spans)
    smem = pl.BlockSpec(memory_space=pltpu.SMEM)
    vmem = pl.BlockSpec(memory_space=pltpu.VMEM)
    hbm = pl.BlockSpec(memory_space=pl.ANY)

    def kernel(*refs):
        forward_kernel(group, spans, *refs)

    if group:
        out_shape = [jax.ShapeDtypeStruct((row_tiles // 2, tile, fin), BF16)] * 2
    else:
        out_shape = [jax.ShapeDtypeStruct((row_tiles + 1, tile, fin), F32)]
    return pl.pallas_call(
        kernel,
        out_shape=out_shape,
        in_specs=[smem] * 2 + [vmem] + [hbm] * len(pieces) + [vmem] * group,
        out_specs=[vmem] * len(out_shape),
        scratch_shapes=[
            pltpu.VMEM((blocks + 1, tile, fin), BF16),
            pltpu.VMEM((row_tiles + 1, tile, fin), F32),
            pltpu.SemaphoreType.DMA((len(pieces),)),
        ],
        compiler_params=pltpu.CompilerParams(vmem_limit_bytes=VMEM_LIMIT),
        cost_estimate=pl.CostEstimate(
            flops=blocks * 2 * 2 * tile**3, bytes_accessed=blocks * 4 * tile**2, transcendentals=0
        ),
        name="forward_far" if group else "forward_near",
    )(slot_info, member, tiles, *pieces, *([before] if group else []))


def backward_tiles(slots, layout, tiles, backs, outs, rider, acc):
    def one(i):
        c = slots.col(i)
        tile = tiles[slots.slot(i)]
        acc[c] = acc[c] + jnp.dot(backs[slots.row(i)], tile, preferred_element_type=F32)

    slots.each(one)
    size = acc.shape[0] // len(layout)
    for i, kind in enumerate(layout):
        outs[i][pl.ds(0, size)] = acc[pl.ds(i * size, size)].astype(BF16)
        if kind:
            extra = rider[...] if kind == "rider" else jnp.zeros_like(outs[i][pl.ds(size, 1)])
            outs[i][pl.ds(size, 1)] = extra


def piece_shapes(layout, size, fin, tile):
    return [
        jax.ShapeDtypeStruct((size + 1 if kind else size, fin, tile), BF16) for kind in layout
    ]


def backward_far_kernel(
    layout, slots_ref, member_ref, tiles, sum_a, sum_b, c0, c1, c2, c3, weight,
    out, rider, backs, *refs,
):
    n = len(layout)
    outs = refs[:n]
    acc, agg, gpre, wfull = refs[n:]
    member = member_ref[0]
    slots = Slots(slots_ref, 1)
    half, tile, fin = sum_a.shape
    node_dev = out.shape[0]
    per_dev = node_dev // tile
    nodes = half * tile
    for source, which in ((sum_a, member % 2), (sum_b, 1 - member % 2)):
        part = pl.ds(pl.multiple_of(which * nodes, nodes), nodes)
        agg[part, :] = source[...].reshape(nodes, fin)
    acc[...] = jnp.zeros_like(acc)
    for d, cot in enumerate((c0, c1, c2, c3)):
        who = member ^ d
        at = pl.multiple_of(who * node_dev, node_dev)
        mine = agg[pl.ds(at, node_dev), :]
        pre = jnp.dot(mine, weight[...], preferred_element_type=F32)
        sig = jax.nn.sigmoid(pre)
        if d == 0:
            out[...] = (pre * sig).astype(BF16)
        grad = (cot[...].astype(F32) * sig * (1.0 + pre * (1.0 - sig))).astype(BF16)
        gpre[pl.ds(at, node_dev), :] = grad
        back = lax.dot_general(
            weight[...], grad, (((1,), (1,)), ((), ())), preferred_element_type=F32
        ).astype(BF16)
        for j in range(per_dev):
            backs[who * per_dev + j] = back[:, j * tile : (j + 1) * tile]
    backs[backs.shape[0] - 1] = jnp.zeros(backs.shape[1:], BF16)
    wfull[...] = lax.dot_general(
        agg[...], gpre[...], (((0,), (0,)), ((), ())), preferred_element_type=F32
    )
    fin, fout = wfull.shape
    share = fin // 2
    part = wfull[pl.ds(pl.multiple_of(member % 2 * share, share), share), :].astype(BF16)
    rider[0, pl.ds(0, share), :] = part[:, : fout // 2]
    rider[0, pl.ds(share, share), :] = part[:, fout // 2 :]
    backward_tiles(slots, layout, tiles, backs, outs, rider, acc)


def backward_far_call(slot_info, member, tiles, sum_a, sum_b, cots, weight, size):
    tile = tiles.shape[-1]
    half, _, fin = sum_a.shape
    row_tiles = 2 * half
    node_dev, fout = cots[0].shape
    nodes = row_tiles * tile
    layout = (None, "rider", None, "rider", None, "none")
    blocks = size * len(layout)
    smem = pl.BlockSpec(memory_space=pltpu.SMEM)
    vmem = pl.BlockSpec(memory_space=pltpu.VMEM)

    def kernel(*refs):
        backward_far_kernel(layout, *refs)

    return pl.pallas_call(
        kernel,
        out_shape=[
            jax.ShapeDtypeStruct((node_dev, fout), BF16),
            jax.ShapeDtypeStruct((1, fin, tile), BF16),
            jax.ShapeDtypeStruct((row_tiles + 1, fin, tile), BF16),
            *piece_shapes(layout, size, fin, tile),
        ],
        in_specs=[smem] * 2 + [vmem] * 8,
        out_specs=[vmem] * (3 + len(layout)),
        scratch_shapes=[
            pltpu.VMEM((blocks + 1, fin, tile), F32),
            pltpu.VMEM((nodes, fin), BF16),
            pltpu.VMEM((nodes, fout), BF16),
            pltpu.VMEM((fin, fout), F32),
        ],
        compiler_params=pltpu.CompilerParams(vmem_limit_bytes=VMEM_LIMIT),
        cost_estimate=pl.CostEstimate(
            flops=blocks * 2 * 2 * tile**3, bytes_accessed=blocks * 6 * tile**2, transcendentals=0
        ),
        name="dense_and_backward_far",
    )(slot_info, member, tiles, sum_a, sum_b, *cots, weight)


def backward_near_kernel(layout, slots_ref, tiles, backs, *refs):
    n = len(layout)
    outs = refs[:n]
    (acc,) = refs[n:]
    slots = Slots(slots_ref, 0)
    acc[...] = jnp.zeros_like(acc)
    backward_tiles(slots, layout, tiles, backs, outs, None, acc)


def backward_near_call(slot_info, tiles, backs, size):
    tile = tiles.shape[-1]
    fin = backs.shape[1]
    layout = (None, None) + (None, "none") * 4
    blocks = size * len(layout)
    smem = pl.BlockSpec(memory_space=pltpu.SMEM)
    vmem = pl.BlockSpec(memory_space=pltpu.VMEM)

    def kernel(*refs):
        backward_near_kernel(layout, *refs)

    return pl.pallas_call(
        kernel,
        out_shape=piece_shapes(layout, size, fin, tile),
        in_specs=[smem, vmem, vmem],
        out_specs=[vmem] * len(layout),
        scratch_shapes=[
            pltpu.VMEM((blocks + 1, fin, tile), F32),
        ],
        compiler_params=pltpu.CompilerParams(vmem_limit_bytes=VMEM_LIMIT),
        cost_estimate=pl.CostEstimate(
            flops=blocks * 2 * 2 * tile**3, bytes_accessed=blocks * 6 * tile**2, transcendentals=0
        ),
        name="backward_near",
    )(slot_info, tiles, backs)


def gather_features(features, cotangent, slot_info, tile, near_call):
    fin = features.shape[1]
    mine = features.reshape(-1, tile, fin)
    other, cot1 = fence(send(mine, dx=1), send_team(cotangent, 1))
    own = join(mine, other)
    y1 = send(own, dy=-1)
    y3 = send(own, dy=1)
    y2 = send(own, dy=-2)
    y1, y3, slot_info = fence(y1, y3, slot_info)
    up0, up1 = [join(own, y1)], [join(y2, y3)]
    down0, down1 = [up0[0]], [up1[0]]
    for step in range(4):
        up0.append(send(up0[-1], dz=-1))
        down1.append(send(down1[-1], dz=1))
        if step < 3:
            down0.append(send(down0[-1], dz=1))
            up1.append(send(up1[-1], dz=-1))
    cot2 = send_team(cotangent, 2)
    cot3 = send_team(cot1, 2)
    near = [up0[0], up1[0], up0[1], up1[1], up0[2], up1[2]]
    near += [down0[2], down1[2], down0[1], down1[1]]
    near_sum = near_call(slot_info, near)
    near_sum, cot2, cot3 = fence(near_sum, cot2, cot3)
    far = [up0[3], up1[3], up0[4], down1[4], down0[3], down1[3]]
    return near_sum, far, (cotangent, cot1, cot2, cot3), slot_info


def spans_of(pieces):
    spans, at = [], 0
    for piece in pieces:
        spans.append((at, piece.shape[0]))
        at += piece.shape[0]
    return spans


def add_pair(a, b, c, d):
    vmem = pl.BlockSpec(memory_space=pltpu.VMEM)

    def kernel(a_ref, b_ref, c_ref, d_ref, ab_ref, cd_ref):
        for x, y, out in ((a_ref, b_ref, ab_ref), (c_ref, d_ref, cd_ref)):
            out[...] = (x[...].astype(F32) + y[...].astype(F32)).astype(BF16)

    return pl.pallas_call(
        kernel,
        out_shape=[jax.ShapeDtypeStruct(a.shape, BF16), jax.ShapeDtypeStruct(c.shape, BF16)],
        in_specs=[vmem] * 4,
        out_specs=[vmem] * 2,
        compiler_params=pltpu.CompilerParams(vmem_limit_bytes=8 * 2**20),
        name="add_pair",
    )(a, b, c, d)


def ring_sums(arrived, long, short, dz):
    ahead, back = [arrived], []
    for i, (term, other) in enumerate(zip(long, short)):
        if i:
            message, reply = add_pair(term, ahead[-1], other, back[-1])
        else:
            message, reply = add(term, ahead[-1]).astype(BF16), other
        message, reply = fence(send(message, dz=dz), send(reply, dz=-dz))
        ahead.append(message)
        back.append(reply)
    return ahead, back


def scatter_sums(near_call, far, rider):
    g3, g4, g5 = [far[2 * i : 2 * i + 2] for i in range(3)]
    first0, first1 = send(g4[0], dz=1), send(g4[1], dz=-1)
    first0, *near = fence(first0, *near_call())
    g0, g1, g2, g6, g7 = [near[2 * i : 2 * i + 2] for i in range(5)]
    up0, down0 = ring_sums(first0, (g3[0], g2[0], g1[0]), (g5[0], g6[0], g7[0]), 1)
    down1, up1 = ring_sums(first1, (g5[1], g6[1], g7[1]), (g3[1], g2[1], g1[1]), -1)
    size = g0[0].shape[0]
    plane0 = add(g0[0], up0[-1], down0[-1])
    plane1 = add(g0[1], up1[-1][:size], down1[-1][:size]).astype(BF16)
    u1, u2, u3 = [part[size:] for part in up1]
    d1, d2, d3, d4 = [part[size:] for part in down1]
    rider = ((add(rider, d4) + add(u2, d2)) + (add(u1, d3) + add(u3, d1))).astype(BF16)
    half = size // 2
    got1 = send(join(plane0[half:].astype(BF16), rider), dy=1)
    got2 = send(join(plane1[:half], rider), dy=2)
    got3 = send(join(plane1[half:], rider), dy=-1)
    line = add(plane0[:half], got1[:half], got2[:half], got3[:half])
    rider = (add(rider, got2[half:]) + add(got1[half:], got3[half:])).astype(BF16)
    size = half
    half = size // 2
    got = send(join(line[half:].astype(BF16), rider), dx=1)
    total = add(line[:half], got[:half])
    weight = add(rider, got[half:])[0]
    share = weight.shape[0] // 2
    weight = jnp.concatenate([weight[:share], weight[share:]], axis=1)
    other = send_team(weight, 1)
    low = lax.axis_index("team") % 2 == 0
    return total, jnp.where(low, join(weight, other), join(other, weight))


def per_device(features, weight, tiles, tile_rows, tile_cols, tile_count, cotangent):
    node_dev, fin = features.shape
    tile = tiles.shape[-1]
    slots = tiles.shape[2]
    sections = lax.axis_size("section")
    teams = lax.axis_size("team")
    row_tiles = node_dev // tile * teams
    scale = 1.0 / math.sqrt(node_dev * sections * teams)
    slab = tiles.reshape(slots, tile, tile)
    slot_info = sort_slots(
        tile_rows.reshape(slots),
        tile_cols.reshape(slots),
        tile_count.reshape(()),
        lax.axis_index("section"),
        row_tiles,
    )
    member = lax.axis_index("team").astype(jnp.int32).reshape(1)


    def near_call(info, pieces):
        return forward_call(0, info, member, slab, pieces, spans_of(pieces), None, row_tiles)[0]

    near_sum, far, cots, slot_info = gather_features(
        features, cotangent, slot_info, tile, near_call
    )
    mine, theirs = forward_call(
        1, slot_info, member, slab, far, spans_of(far), near_sum, row_tiles
    )
    pair = add(mine, send_team(theirs, 1)).astype(BF16)
    mine = add(pair, send_team(pair, 2)).astype(BF16)
    size = far[0].shape[0]
    output, rider, backs, *far_terms = backward_far_call(
        slot_info, member, slab, mine, send_team(mine, 1), cots, weight, size
    )
    total, weight_sum = scatter_sums(
        lambda: backward_near_call(slot_info, slab, backs, size), far_terms, rider
    )
    grad_features = total.transpose(0, 2, 1).reshape(node_dev, fin).astype(BF16)
    return output, grad_features, weight_sum * scale


def solution(mesh):
    in_specs = (
        P(("section", "team"), None),
        P(),
        P("section", "team", None, None, None),
        P("section", "team", None),
        P("section", "team", None),
        P("section", "team"),
        P(("section", "team"), None),
    )
    out_specs = (P(("section", "team"), None), P(("section", "team"), None), P())
    return jax.shard_map(
        per_device, mesh=mesh, in_specs=in_specs, out_specs=out_specs, check_vma=False
    )
```

```python
import math

import jax
import jax.numpy as jnp
from jax import lax
from jax.experimental import pallas as pl
from jax.experimental.pallas import tpu as pltpu
from jax.sharding import PartitionSpec as P

NX, NY, NZ = 2, 4, 8
UNROLL = 16
NEAR = (0, 1, 2, 6, 7)
FAR = (3, 4, 5)
F32 = jnp.float32
BF16 = jnp.bfloat16
VMEM_LIMIT = 24 * 2**20


def section_index(x, y, z):
    return ((x % NX) * NY + y % NY) * NZ + z % NZ


def send(value, dx=0, dy=0, dz=0):
    pairs = [
        (section_index(x, y, z), section_index(x + dx, y + dy, z + dz))
        for x in range(NX)
        for y in range(NY)
        for z in range(NZ)
    ]
    return lax.ppermute(value, "section", pairs)


def send_team(value, mask):
    return lax.ppermute(value, "team", [(t, t ^ mask) for t in range(4)])


def fence(*arrays):
    return lax.optimization_barrier(arrays)


def add(*terms):
    total = terms[0].astype(F32)
    for term in terms[1:]:
        total = total + term.astype(F32)
    return total


def join(*arrays):
    return jnp.concatenate(arrays)


def sort_kernel(row_tiles, keys, out):
    slots = keys.shape[0]
    region = slots + UNROLL
    blocks = NY * NX * 2

    def body(step, carry):
        near_n, far_n = carry
        for j in range(8):
            key = keys[step * 8 + j]
            is_near = (key >> 24) & 1
            is_far = key >> 25
            spot = jnp.where(is_far == 1, region + far_n, near_n)
            out[jnp.where(is_near + is_far == 1, spot, 2 * region)] = key
            near_n = near_n + is_near
            far_n = far_n + is_far
        return near_n, far_n

    zero = jnp.int32(0)
    near_n, far_n = lax.fori_loop(0, slots // 8, body, (zero, zero))
    for j in range(UNROLL):
        out[near_n + j] = (row_tiles << 8) + (len(NEAR) * blocks << 12)
        out[region + far_n + j] = (row_tiles << 8) + (len(FAR) * blocks << 12)
    out[2 * region + UNROLL] = (near_n + UNROLL - 1) // UNROLL
    out[2 * region + UNROLL + 1] = (far_n + UNROLL - 1) // UNROLL


def slot_keys(rows, cols, count, me):
    slots = rows.shape[0]
    blocks = NY * NX * 2
    owner = cols // 2
    dx = (owner // (NY * NZ)) ^ (me // (NY * NZ))
    dy = (owner // NZ - me // NZ) % NY
    dz = (owner - me) % NZ
    far = (dz >= FAR[0]) & (dz <= FAR[-1])
    place = jnp.where(dz < FAR[0], dz, dz - FAR[0]) * blocks + dy * (NX * 2) + dx * 2 + cols % 2
    ids = jnp.arange(slots, dtype=jnp.int32)
    group = jnp.where(ids < count, jnp.where(far, 2, 1), 0)
    return (ids + (rows << 8) + (place << 12) + (group << 24)).astype(jnp.int32)


def sort_slots(keys, row_tiles):
    slots = keys.shape[0]
    smem = pl.BlockSpec(memory_space=pltpu.SMEM)

    def kernel(*refs):
        sort_kernel(row_tiles, *refs)

    return pl.pallas_call(
        kernel,
        out_shape=jax.ShapeDtypeStruct((2 * (slots + UNROLL) + UNROLL + 2,), jnp.int32),
        in_specs=[smem],
        out_specs=smem,
        cost_estimate=pl.CostEstimate(flops=4 * 10**9, bytes_accessed=4096, transcendentals=0),
        name="sort_slots",
    )(keys)


class Slots:
    def __init__(self, ref, group):
        self.ref = ref
        length = ref.shape[0] - 2
        self.start = group * ((length - UNROLL) // 2)
        self.chunks = ref[length + group]

    def slot(self, i):
        return self.ref[self.start + i] & 255

    def row(self, i):
        return (self.ref[self.start + i] >> 8) & 15

    def col(self, i):
        return (self.ref[self.start + i] >> 12) & 255

    def each(self, fn):
        def body(c, carry):
            for j in range(UNROLL):
                fn(c * UNROLL + j)
            return carry

        lax.fori_loop(0, self.chunks, body, 0)


def forward_kernel(group, spans, slots_ref, member_ref, tiles, *refs):
    n = len(spans)
    pieces = refs[:n]
    before = refs[n] if group else None
    *outs, feat, acc = refs[n + group :]
    slots = Slots(slots_ref, group)
    for piece, (at, size) in zip(pieces, spans):
        feat[pl.ds(at, size)] = piece[...]
    acc[...] = before[...] if group else jnp.zeros_like(acc)
    feat[feat.shape[0] - 1] = jnp.zeros(feat.shape[1:], feat.dtype)

    def one(i):
        r = slots.row(i)
        tile = tiles[slots.slot(i)]
        acc[r] = acc[r] + jnp.dot(tile, feat[slots.col(i)], preferred_element_type=F32)

    slots.each(one)
    if group:
        half = outs[0].shape[0]
        core = member_ref[0] % 2
        outs[0][...] = acc[pl.ds(core * half, half)].astype(BF16)
        outs[1][...] = acc[pl.ds((1 - core) * half, half)].astype(BF16)
    else:
        outs[0][...] = acc[...]


def forward_call(group, slot_info, member, tiles, pieces, spans, before, row_tiles):
    tile = tiles.shape[-1]
    fin = pieces[0].shape[-1]
    blocks = sum(size for _, size in spans)
    smem = pl.BlockSpec(memory_space=pltpu.SMEM)
    vmem = pl.BlockSpec(memory_space=pltpu.VMEM)

    def kernel(*refs):
        forward_kernel(group, spans, *refs)

    if group:
        out_shape = [jax.ShapeDtypeStruct((row_tiles // 2, tile, fin), BF16)] * 2
    else:
        out_shape = [jax.ShapeDtypeStruct((row_tiles + 1, tile, fin), F32)]
    return pl.pallas_call(
        kernel,
        out_shape=out_shape,
        in_specs=[smem] * 2 + [vmem] * (1 + len(pieces) + group),
        out_specs=[vmem] * len(out_shape),
        scratch_shapes=[
            pltpu.VMEM((blocks + 1, tile, fin), BF16),
            pltpu.VMEM((row_tiles + 1, tile, fin), F32),
        ],
        compiler_params=pltpu.CompilerParams(vmem_limit_bytes=VMEM_LIMIT),
        cost_estimate=pl.CostEstimate(
            flops=blocks * 2 * 2 * tile**3, bytes_accessed=blocks * 4 * tile**2, transcendentals=0
        ),
        name="forward_far" if group else "forward_near",
    )(slot_info, member, tiles, *pieces, *([before] if group else []))


def backward_tiles(slots, layout, tiles, backs, outs, rider, acc):
    def one(i):
        c = slots.col(i)
        tile = tiles[slots.slot(i)]
        acc[c] = acc[c] + jnp.dot(backs[slots.row(i)], tile, preferred_element_type=F32)

    slots.each(one)
    size = acc.shape[0] // len(layout)
    for i, kind in enumerate(layout):
        outs[i][pl.ds(0, size)] = acc[pl.ds(i * size, size)].astype(BF16)
        if kind:
            extra = rider[...] if kind == "rider" else jnp.zeros_like(outs[i][pl.ds(size, 1)])
            outs[i][pl.ds(size, 1)] = extra


def piece_shapes(layout, size, fin, tile):
    return [
        jax.ShapeDtypeStruct((size + 1 if kind else size, fin, tile), BF16) for kind in layout
    ]


def backward_far_kernel(
    layout, slots_ref, member_ref, tiles, sum_a, sum_b, c0, c1, c2, c3, weight,
    out, rider, backs, *refs,
):
    n = len(layout)
    outs = refs[:n]
    acc, agg, gpre, wfull = refs[n:]
    member = member_ref[0]
    slots = Slots(slots_ref, 1)
    half, tile, fin = sum_a.shape
    node_dev = out.shape[0]
    per_dev = node_dev // tile
    nodes = half * tile
    for source, which in ((sum_a, member % 2), (sum_b, 1 - member % 2)):
        part = pl.ds(pl.multiple_of(which * nodes, nodes), nodes)
        agg[part, :] = source[...].reshape(nodes, fin)
    acc[...] = jnp.zeros_like(acc)
    for d, cot in enumerate((c0, c1, c2, c3)):
        who = member ^ d
        at = pl.multiple_of(who * node_dev, node_dev)
        mine = agg[pl.ds(at, node_dev), :]
        pre = jnp.dot(mine, weight[...], preferred_element_type=F32)
        sig = jax.nn.sigmoid(pre)
        if d == 0:
            out[...] = (pre * sig).astype(BF16)
        grad = (cot[...].astype(F32) * sig * (1.0 + pre * (1.0 - sig))).astype(BF16)
        gpre[pl.ds(at, node_dev), :] = grad
        back = lax.dot_general(
            weight[...], grad, (((1,), (1,)), ((), ())), preferred_element_type=F32
        ).astype(BF16)
        for j in range(per_dev):
            backs[who * per_dev + j] = back[:, j * tile : (j + 1) * tile]
    backs[backs.shape[0] - 1] = jnp.zeros(backs.shape[1:], BF16)
    wfull[...] = lax.dot_general(
        agg[...], gpre[...], (((0,), (0,)), ((), ())), preferred_element_type=F32
    )
    fin, fout = wfull.shape
    share = fin // 2
    part = wfull[pl.ds(pl.multiple_of(member % 2 * share, share), share), :].astype(BF16)
    rider[0, pl.ds(0, share), :] = part[:, : fout // 2]
    rider[0, pl.ds(share, share), :] = part[:, fout // 2 :]
    backward_tiles(slots, layout, tiles, backs, outs, rider, acc)


def backward_far_call(slot_info, member, tiles, sum_a, sum_b, cots, weight, size):
    tile = tiles.shape[-1]
    half, _, fin = sum_a.shape
    row_tiles = 2 * half
    node_dev, fout = cots[0].shape
    nodes = row_tiles * tile
    layout = ("none", None, "rider", None, "rider", None)
    blocks = size * len(layout)
    smem = pl.BlockSpec(memory_space=pltpu.SMEM)
    vmem = pl.BlockSpec(memory_space=pltpu.VMEM)

    def kernel(*refs):
        backward_far_kernel(layout, *refs)

    return pl.pallas_call(
        kernel,
        out_shape=[
            jax.ShapeDtypeStruct((node_dev, fout), BF16),
            jax.ShapeDtypeStruct((1, fin, tile), BF16),
            jax.ShapeDtypeStruct((row_tiles + 1, fin, tile), BF16),
            *piece_shapes(layout, size, fin, tile),
        ],
        in_specs=[smem] * 2 + [vmem] * 8,
        out_specs=[vmem] * (3 + len(layout)),
        scratch_shapes=[
            pltpu.VMEM((blocks + 1, fin, tile), F32),
            pltpu.VMEM((nodes, fin), BF16),
            pltpu.VMEM((nodes, fout), BF16),
            pltpu.VMEM((fin, fout), F32),
        ],
        compiler_params=pltpu.CompilerParams(vmem_limit_bytes=VMEM_LIMIT),
        cost_estimate=pl.CostEstimate(
            flops=blocks * 2 * 2 * tile**3, bytes_accessed=blocks * 6 * tile**2, transcendentals=0
        ),
        name="dense_and_backward_far",
    )(slot_info, member, tiles, sum_a, sum_b, *cots, weight)


def backward_near_kernel(layout, slots_ref, tiles, backs, *refs):
    n = len(layout)
    outs = refs[:n]
    (acc,) = refs[n:]
    slots = Slots(slots_ref, 0)
    acc[...] = jnp.zeros_like(acc)
    backward_tiles(slots, layout, tiles, backs, outs, None, acc)


def backward_near_call(slot_info, tiles, backs, size):
    tile = tiles.shape[-1]
    fin = backs.shape[1]
    layout = (None, None) + ("none", None) * 4
    blocks = size * len(layout)
    smem = pl.BlockSpec(memory_space=pltpu.SMEM)
    vmem = pl.BlockSpec(memory_space=pltpu.VMEM)

    def kernel(*refs):
        backward_near_kernel(layout, *refs)

    return pl.pallas_call(
        kernel,
        out_shape=piece_shapes(layout, size, fin, tile),
        in_specs=[smem, vmem, vmem],
        out_specs=[vmem] * len(layout),
        scratch_shapes=[
            pltpu.VMEM((blocks + 1, fin, tile), F32),
        ],
        compiler_params=pltpu.CompilerParams(vmem_limit_bytes=VMEM_LIMIT),
        cost_estimate=pl.CostEstimate(
            flops=blocks * 2 * 2 * tile**3, bytes_accessed=blocks * 6 * tile**2, transcendentals=0
        ),
        name="backward_near",
    )(slot_info, tiles, backs)


def gather_features(features, cotangent, keys, row_tiles, tile, near_call):
    fin = features.shape[1]
    mine = features.reshape(-1, tile, fin)
    other, cot1, keys = fence(send(mine, dx=1), send_team(cotangent, 1), keys)
    own = join(mine, other)
    y1 = send(own, dy=-1)
    y3 = send(own, dy=1)
    y2 = send(own, dy=-2)
    up0, up1 = [join(own, y1)], [join(y2, y3)]
    down0, down1 = [up0[0]], [up1[0]]
    for step in range(4):
        up0.append(send(up0[-1], dz=-1))
        if step == 0:
            up0[1], slot_info = fence(up0[1], sort_slots(keys, row_tiles))
        down1.append(send(down1[-1], dz=1))
        if step < 3:
            down0.append(send(down0[-1], dz=1))
            up1.append(send(up1[-1], dz=-1))
    cot2 = send_team(cotangent, 2)
    cot3 = send_team(cot1, 2)
    near = [up0[0], up1[0], up0[1], up1[1], up0[2], up1[2]]
    near += [down0[2], down1[2], down0[1], down1[1]]
    near_sum = near_call(slot_info, near)
    near_sum, cot2, cot3 = fence(near_sum, cot2, cot3)
    far = [up0[3], up1[3], up0[4], down1[4], down0[3], down1[3]]
    return near_sum, far, (cotangent, cot1, cot2, cot3), slot_info


def spans_of(pieces):
    spans, at = [], 0
    for piece in pieces:
        spans.append((at, piece.shape[0]))
        at += piece.shape[0]
    return spans


def add_pair(a, b, c, d):
    vmem = pl.BlockSpec(memory_space=pltpu.VMEM)

    def kernel(a_ref, b_ref, c_ref, d_ref, ab_ref, cd_ref):
        for x, y, out in ((a_ref, b_ref, ab_ref), (c_ref, d_ref, cd_ref)):
            out[...] = (x[...].astype(F32) + y[...].astype(F32)).astype(BF16)

    return pl.pallas_call(
        kernel,
        out_shape=[jax.ShapeDtypeStruct(a.shape, BF16), jax.ShapeDtypeStruct(c.shape, BF16)],
        in_specs=[vmem] * 4,
        out_specs=[vmem] * 2,
        compiler_params=pltpu.CompilerParams(vmem_limit_bytes=8 * 2**20),
        name="add_pair",
    )(a, b, c, d)


def ring_sums(long, short, dz):
    ahead, back = [], []
    message, reply = long[0], short[0]
    for i in range(len(short)):
        if i:
            message, reply = add_pair(long[i], ahead[-1], short[i], back[-1])
        message, reply = fence(send(message, dz=dz), send(reply, dz=-dz))
        ahead.append(message)
        back.append(reply)
    ahead.append(send(add(long[-1], ahead[-1]).astype(BF16), dz=dz))
    return ahead, back


def scatter_sums(near, far, rider):
    g3, g4, g5 = [far[2 * i : 2 * i + 2] for i in range(3)]
    g0, g1, g2, g6, g7 = [near[2 * i : 2 * i + 2] for i in range(5)]
    up0, down0 = ring_sums((g4[0], g3[0], g2[0], g1[0]), (g5[0], g6[0], g7[0]), 1)
    down1, up1 = ring_sums((g4[1], g5[1], g6[1], g7[1]), (g3[1], g2[1], g1[1]), -1)
    size = g0[0].shape[0]
    plane0 = add(g0[0], up0[-1][:size], down0[-1][:size])
    plane1 = add(g0[1], up1[-1], down1[-1]).astype(BF16)
    u1, u2, u3, u4 = [part[size:] for part in up0]
    d1, d2, d3 = [part[size:] for part in down0]
    rider = ((add(rider, u4) + add(u2, d2)) + (add(u1, d3) + add(u3, d1))).astype(BF16)
    half = size // 2
    got1 = send(join(plane0[half:].astype(BF16), rider), dy=1)
    got2 = send(join(plane1[:half], rider), dy=2)
    got3 = send(join(plane1[half:], rider), dy=-1)
    line = add(plane0[:half], got1[:half], got2[:half], got3[:half])
    rider = (add(rider, got2[half:]) + add(got1[half:], got3[half:])).astype(BF16)
    size = half
    half = size // 2
    got = send(join(line[half:].astype(BF16), rider), dx=1)
    total = add(line[:half], got[:half])
    weight = add(rider, got[half:])[0]
    share = weight.shape[0] // 2
    weight = jnp.concatenate([weight[:share], weight[share:]], axis=1)
    other = send_team(weight, 1)
    low = lax.axis_index("team") % 2 == 0
    return total, jnp.where(low, join(weight, other), join(other, weight))


def per_device(features, weight, tiles, tile_rows, tile_cols, tile_count, cotangent):
    node_dev, fin = features.shape
    tile = tiles.shape[-1]
    slots = tiles.shape[2]
    sections = lax.axis_size("section")
    teams = lax.axis_size("team")
    row_tiles = node_dev // tile * teams
    scale = 1.0 / math.sqrt(node_dev * sections * teams)
    slab = tiles.reshape(slots, tile, tile)
    keys = slot_keys(
        tile_rows.reshape(slots),
        tile_cols.reshape(slots),
        tile_count.reshape(()),
        lax.axis_index("section"),
    )
    member = lax.axis_index("team").astype(jnp.int32).reshape(1)


    def near_call(info, pieces):
        return forward_call(0, info, member, slab, pieces, spans_of(pieces), None, row_tiles)[0]

    near_sum, far, cots, slot_info = gather_features(
        features, cotangent, keys, row_tiles, tile, near_call
    )
    mine, theirs = forward_call(
        1, slot_info, member, slab, far, spans_of(far), near_sum, row_tiles
    )
    pair = add(mine, send_team(theirs, 1)).astype(BF16)
    mine = add(pair, send_team(pair, 2)).astype(BF16)
    size = far[0].shape[0]
    output, rider, backs, *far_terms = backward_far_call(
        slot_info, member, slab, mine, send_team(mine, 1), cots, weight, size
    )
    near_terms = backward_near_call(slot_info, slab, backs, size)
    total, weight_sum = scatter_sums(near_terms, far_terms, rider)
    grad_features = total.transpose(0, 2, 1).reshape(node_dev, fin).astype(BF16)
    return output, grad_features, weight_sum * scale


def solution(mesh):
    in_specs = (
        P(("section", "team"), None),
        P(),
        P("section", "team", None, None, None),
        P("section", "team", None),
        P("section", "team", None),
        P("section", "team"),
        P(("section", "team"), None),
    )
    out_specs = (P(("section", "team"), None), P(("section", "team"), None), P())
    return jax.shard_map(
        per_device, mesh=mesh, in_specs=in_specs, out_specs=out_specs, check_vma=False
    )
```

```python
import math

import jax
import jax.numpy as jnp
from jax import lax
from jax.experimental import pallas as pl
from jax.experimental.pallas import tpu as pltpu
from jax.sharding import PartitionSpec as P

NX, NY, NZ = 2, 4, 8
UNROLL = 16
NEAR = (0, 1, 2, 6, 7)
FAR = (3, 4, 5)
F32 = jnp.float32
BF16 = jnp.bfloat16
VMEM_LIMIT = 24 * 2**20


def section_index(x, y, z):
    return ((x % NX) * NY + y % NY) * NZ + z % NZ


def send(value, dx=0, dy=0, dz=0):
    pairs = [
        (section_index(x, y, z), section_index(x + dx, y + dy, z + dz))
        for x in range(NX)
        for y in range(NY)
        for z in range(NZ)
    ]
    return lax.ppermute(value, "section", pairs)


def send_team(value, mask):
    return lax.ppermute(value, "team", [(t, t ^ mask) for t in range(4)])


def fence(*arrays):
    return lax.optimization_barrier(arrays)


def add(*terms):
    total = terms[0].astype(F32)
    for term in terms[1:]:
        total = total + term.astype(F32)
    return total


def join(*arrays):
    return jnp.concatenate(arrays)


def sort_kernel(row_tiles, keys, out):
    slots = keys.shape[0]
    region = slots + UNROLL
    blocks = NY * NX * 2

    def body(step, carry):
        near_n, far_n = carry
        for j in range(8):
            key = keys[step * 8 + j]
            is_near = (key >> 24) & 1
            is_far = key >> 25
            spot = jnp.where(is_far == 1, region + far_n, near_n)
            out[jnp.where(is_near + is_far == 1, spot, 2 * region)] = key
            near_n = near_n + is_near
            far_n = far_n + is_far
        return near_n, far_n

    zero = jnp.int32(0)
    near_n, far_n = lax.fori_loop(0, slots // 8, body, (zero, zero))
    for j in range(UNROLL):
        out[near_n + j] = (row_tiles << 8) + (len(NEAR) * blocks << 12)
        out[region + far_n + j] = (row_tiles << 8) + (len(FAR) * blocks << 12)
    out[2 * region + UNROLL] = (near_n + UNROLL - 1) // UNROLL
    out[2 * region + UNROLL + 1] = (far_n + UNROLL - 1) // UNROLL


def slot_keys(rows, cols, count, me):
    slots = rows.shape[0]
    blocks = NY * NX * 2
    owner = cols // 2
    dx = (owner // (NY * NZ)) ^ (me // (NY * NZ))
    dy = (owner // NZ - me // NZ) % NY
    dz = (owner - me) % NZ
    far = (dz >= FAR[0]) & (dz <= FAR[-1])
    place = jnp.where(dz < FAR[0], dz, dz - FAR[0]) * blocks + dy * (NX * 2) + dx * 2 + cols % 2
    ids = jnp.arange(slots, dtype=jnp.int32)
    group = jnp.where(ids < count, jnp.where(far, 2, 1), 0)
    return (ids + (rows << 8) + (place << 12) + (group << 24)).astype(jnp.int32)


def sort_slots(keys, row_tiles):
    slots = keys.shape[0]
    smem = pl.BlockSpec(memory_space=pltpu.SMEM)

    def kernel(*refs):
        sort_kernel(row_tiles, *refs)

    return pl.pallas_call(
        kernel,
        out_shape=jax.ShapeDtypeStruct((2 * (slots + UNROLL) + UNROLL + 2,), jnp.int32),
        in_specs=[smem],
        out_specs=smem,
        cost_estimate=pl.CostEstimate(flops=4 * 10**9, bytes_accessed=4096, transcendentals=0),
        name="sort_slots",
    )(keys)


class Slots:
    def __init__(self, ref, group):
        self.ref = ref
        length = ref.shape[0] - 2
        self.start = group * ((length - UNROLL) // 2)
        self.chunks = ref[length + group]

    def slot(self, i):
        return self.ref[self.start + i] & 255

    def row(self, i):
        return (self.ref[self.start + i] >> 8) & 15

    def col(self, i):
        return (self.ref[self.start + i] >> 12) & 255

    def each(self, fn):
        def body(c, carry):
            for j in range(UNROLL):
                fn(c * UNROLL + j)
            return carry

        lax.fori_loop(0, self.chunks, body, 0)


def forward_kernel(group, spans, slots_ref, member_ref, tiles, *refs):
    n = len(spans)
    pieces = refs[:n]
    before = refs[n] if group else None
    *outs, feat, acc = refs[n + group :]
    slots = Slots(slots_ref, group)
    for piece, (at, size) in zip(pieces, spans):
        feat[pl.ds(at, size)] = piece[...]
    acc[...] = before[...] if group else jnp.zeros_like(acc)
    feat[feat.shape[0] - 1] = jnp.zeros(feat.shape[1:], feat.dtype)

    def one(i):
        r = slots.row(i)
        tile = tiles[slots.slot(i)]
        acc[r] = acc[r] + jnp.dot(tile, feat[slots.col(i)], preferred_element_type=F32)

    slots.each(one)
    if group:
        half = outs[0].shape[0]
        core = member_ref[0] % 2
        outs[0][...] = acc[pl.ds(core * half, half)].astype(BF16)
        outs[1][...] = acc[pl.ds((1 - core) * half, half)].astype(BF16)
    else:
        outs[0][...] = acc[...]


def forward_call(group, slot_info, member, tiles, pieces, spans, before, row_tiles):
    tile = tiles.shape[-1]
    fin = pieces[0].shape[-1]
    blocks = sum(size for _, size in spans)
    smem = pl.BlockSpec(memory_space=pltpu.SMEM)
    vmem = pl.BlockSpec(memory_space=pltpu.VMEM)

    def kernel(*refs):
        forward_kernel(group, spans, *refs)

    if group:
        out_shape = [jax.ShapeDtypeStruct((row_tiles // 2, tile, fin), BF16)] * 2
    else:
        out_shape = [jax.ShapeDtypeStruct((row_tiles + 1, tile, fin), F32)]
    return pl.pallas_call(
        kernel,
        out_shape=out_shape,
        in_specs=[smem] * 2 + [vmem] * (1 + len(pieces) + group),
        out_specs=[vmem] * len(out_shape),
        scratch_shapes=[
            pltpu.VMEM((blocks + 1, tile, fin), BF16),
            pltpu.VMEM((row_tiles + 1, tile, fin), F32),
        ],
        compiler_params=pltpu.CompilerParams(vmem_limit_bytes=VMEM_LIMIT),
        cost_estimate=pl.CostEstimate(
            flops=blocks * 2 * 2 * tile**3, bytes_accessed=blocks * 4 * tile**2, transcendentals=0
        ),
        name="forward_far" if group else "forward_near",
    )(slot_info, member, tiles, *pieces, *([before] if group else []))


def backward_tiles(slots, layout, tiles, backs, outs, rider, acc):
    def one(i):
        c = slots.col(i)
        tile = tiles[slots.slot(i)]
        acc[c] = acc[c] + jnp.dot(backs[slots.row(i)], tile, preferred_element_type=F32)

    slots.each(one)
    size = acc.shape[0] // len(layout)
    for i, kind in enumerate(layout):
        outs[i][pl.ds(0, size)] = acc[pl.ds(i * size, size)].astype(BF16)
        if kind:
            extra = rider[...] if kind == "rider" else jnp.zeros_like(outs[i][pl.ds(size, 1)])
            outs[i][pl.ds(size, 1)] = extra


def piece_shapes(layout, size, fin, tile):
    return [
        jax.ShapeDtypeStruct((size + 1 if kind else size, fin, tile), BF16) for kind in layout
    ]


def backward_far_kernel(
    layout, slots_ref, member_ref, tiles, sum_a, sum_b, c0, c1, c2, c3, weight,
    out, rider, backs, *refs,
):
    n = len(layout)
    outs = refs[:n]
    acc, agg, gpre, wfull = refs[n:]
    member = member_ref[0]
    slots = Slots(slots_ref, 1)
    half, tile, fin = sum_a.shape
    node_dev = out.shape[0]
    per_dev = node_dev // tile
    nodes = half * tile
    for source, which in ((sum_a, member % 2), (sum_b, 1 - member % 2)):
        part = pl.ds(pl.multiple_of(which * nodes, nodes), nodes)
        agg[part, :] = source[...].reshape(nodes, fin)
    acc[...] = jnp.zeros_like(acc)
    for d, cot in enumerate((c0, c1, c2, c3)):
        who = member ^ d
        at = pl.multiple_of(who * node_dev, node_dev)
        mine = agg[pl.ds(at, node_dev), :]
        pre = jnp.dot(mine, weight[...], preferred_element_type=F32)
        sig = jax.nn.sigmoid(pre)
        if d == 0:
            out[...] = (pre * sig).astype(BF16)
        grad = (cot[...].astype(F32) * sig * (1.0 + pre * (1.0 - sig))).astype(BF16)
        gpre[pl.ds(at, node_dev), :] = grad
        back = lax.dot_general(
            weight[...], grad, (((1,), (1,)), ((), ())), preferred_element_type=F32
        ).astype(BF16)
        for j in range(per_dev):
            backs[who * per_dev + j] = back[:, j * tile : (j + 1) * tile]
    backs[backs.shape[0] - 1] = jnp.zeros(backs.shape[1:], BF16)
    wfull[...] = lax.dot_general(
        agg[...], gpre[...], (((0,), (0,)), ((), ())), preferred_element_type=F32
    )
    fin, fout = wfull.shape
    share = fin // 2
    part = wfull[pl.ds(pl.multiple_of(member % 2 * share, share), share), :].astype(BF16)
    rider[0, pl.ds(0, share), :] = part[:, : fout // 2]
    rider[0, pl.ds(share, share), :] = part[:, fout // 2 :]
    backward_tiles(slots, layout, tiles, backs, outs, rider, acc)


def backward_far_call(slot_info, member, tiles, sum_a, sum_b, cots, weight, size):
    tile = tiles.shape[-1]
    half, _, fin = sum_a.shape
    row_tiles = 2 * half
    node_dev, fout = cots[0].shape
    nodes = row_tiles * tile
    layout = ("none", None, "rider", None, "rider", None)
    blocks = size * len(layout)
    smem = pl.BlockSpec(memory_space=pltpu.SMEM)
    vmem = pl.BlockSpec(memory_space=pltpu.VMEM)

    def kernel(*refs):
        backward_far_kernel(layout, *refs)

    return pl.pallas_call(
        kernel,
        out_shape=[
            jax.ShapeDtypeStruct((node_dev, fout), BF16),
            jax.ShapeDtypeStruct((1, fin, tile), BF16),
            jax.ShapeDtypeStruct((row_tiles + 1, fin, tile), BF16),
            *piece_shapes(layout, size, fin, tile),
        ],
        in_specs=[smem] * 2 + [vmem] * 8,
        out_specs=[vmem] * (3 + len(layout)),
        scratch_shapes=[
            pltpu.VMEM((blocks + 1, fin, tile), F32),
            pltpu.VMEM((nodes, fin), BF16),
            pltpu.VMEM((nodes, fout), BF16),
            pltpu.VMEM((fin, fout), F32),
        ],
        compiler_params=pltpu.CompilerParams(vmem_limit_bytes=VMEM_LIMIT),
        cost_estimate=pl.CostEstimate(
            flops=blocks * 2 * 2 * tile**3, bytes_accessed=blocks * 6 * tile**2, transcendentals=0
        ),
        name="dense_and_backward_far",
    )(slot_info, member, tiles, sum_a, sum_b, *cots, weight)


def backward_near_kernel(layout, slots_ref, tiles, backs, *refs):
    n = len(layout)
    outs = refs[:n]
    (acc,) = refs[n:]
    slots = Slots(slots_ref, 0)
    acc[...] = jnp.zeros_like(acc)
    backward_tiles(slots, layout, tiles, backs, outs, None, acc)


def backward_near_call(slot_info, tiles, backs, size):
    tile = tiles.shape[-1]
    fin = backs.shape[1]
    layout = (None, None) + ("none", None) * 4
    blocks = size * len(layout)
    smem = pl.BlockSpec(memory_space=pltpu.SMEM)
    vmem = pl.BlockSpec(memory_space=pltpu.VMEM)

    def kernel(*refs):
        backward_near_kernel(layout, *refs)

    return pl.pallas_call(
        kernel,
        out_shape=piece_shapes(layout, size, fin, tile),
        in_specs=[smem, vmem, vmem],
        out_specs=[vmem] * len(layout),
        scratch_shapes=[
            pltpu.VMEM((blocks + 1, fin, tile), F32),
        ],
        compiler_params=pltpu.CompilerParams(vmem_limit_bytes=VMEM_LIMIT),
        cost_estimate=pl.CostEstimate(
            flops=blocks * 2 * 2 * tile**3, bytes_accessed=blocks * 6 * tile**2, transcendentals=0
        ),
        name="backward_near",
    )(slot_info, tiles, backs)


def gather_features(features, cotangent, keys, row_tiles, tile, near_call):
    fin = features.shape[1]
    mine = features.reshape(-1, tile, fin)
    other, cot1, keys = fence(send(mine, dx=1), send_team(cotangent, 1), keys)
    own = join(mine, other)
    y1 = send(own, dy=-1)
    y3 = send(own, dy=1)
    y2 = send(own, dy=-2)
    up0, up1 = [join(own, y1)], [join(y2, y3)]
    down0, down1 = [up0[0]], [up1[0]]
    for step in range(4):
        up0.append(send(up0[-1], dz=-1))
        if step == 0:
            up0[1], slot_info = fence(up0[1], sort_slots(keys, row_tiles))
        down1.append(send(down1[-1], dz=1))
        if step < 3:
            down0.append(send(down0[-1], dz=1))
            up1.append(send(up1[-1], dz=-1))
    cot2 = send_team(cotangent, 2)
    cot3 = send_team(cot1, 2)
    near = [up0[0], up1[0], up0[1], up1[1], up0[2], up1[2]]
    near += [down0[2], down1[2], down0[1], down1[1]]
    near_sum = near_call(slot_info, near)
    near_sum, cot2, cot3 = fence(near_sum, cot2, cot3)
    far = [up0[3], up1[3], up0[4], down1[4], down0[3], down1[3]]
    return near_sum, far, (cotangent, cot1, cot2, cot3), slot_info


def spans_of(pieces):
    spans, at = [], 0
    for piece in pieces:
        spans.append((at, piece.shape[0]))
        at += piece.shape[0]
    return spans


def add_rounded(a, b):
    vmem = pl.BlockSpec(memory_space=pltpu.VMEM)

    def kernel(a_ref, b_ref, out):
        out[...] = (a_ref[...].astype(F32) + b_ref[...].astype(F32)).astype(BF16)

    return pl.pallas_call(
        kernel,
        out_shape=jax.ShapeDtypeStruct(a.shape, BF16),
        in_specs=[vmem] * 2,
        out_specs=vmem,
        compiler_params=pltpu.CompilerParams(vmem_limit_bytes=8 * 2**20),
        name="add_rounded",
    )(a, b)


def ring_sums(long, short, dz):
    ahead, back = [send(long[0], dz=dz)], [send(short[0], dz=-dz)]
    for i in range(1, len(long)):
        ahead.append(send(add_rounded(long[i], ahead[-1]), dz=dz))
        if i < len(short):
            back.append(send(add_rounded(short[i], back[-1]), dz=-dz))
    return ahead, back


def scatter_sums(near, far, rider):
    g3, g4, g5 = [far[2 * i : 2 * i + 2] for i in range(3)]
    g0, g1, g2, g6, g7 = [near[2 * i : 2 * i + 2] for i in range(5)]
    up0, down0 = ring_sums((g4[0], g3[0], g2[0], g1[0]), (g5[0], g6[0], g7[0]), 1)
    down1, up1 = ring_sums((g4[1], g5[1], g6[1], g7[1]), (g3[1], g2[1], g1[1]), -1)
    size = g0[0].shape[0]
    plane0 = add(g0[0], up0[-1][:size], down0[-1][:size])
    plane1 = add(g0[1], up1[-1], down1[-1]).astype(BF16)
    u1, u2, u3, u4 = [part[size:] for part in up0]
    d1, d2, d3 = [part[size:] for part in down0]
    rider = ((add(rider, u4) + add(u2, d2)) + (add(u1, d3) + add(u3, d1))).astype(BF16)
    half = size // 2
    got1 = send(join(plane0[half:].astype(BF16), rider), dy=1)
    got2 = send(join(plane1[:half], rider), dy=2)
    got3 = send(join(plane1[half:], rider), dy=-1)
    line = add(plane0[:half], got1[:half], got2[:half], got3[:half])
    rider = (add(rider, got2[half:]) + add(got1[half:], got3[half:])).astype(BF16)
    size = half
    half = size // 2
    got = send(join(line[half:].astype(BF16), rider), dx=1)
    total = add(line[:half], got[:half])
    weight = add(rider, got[half:])[0]
    share = weight.shape[0] // 2
    weight = jnp.concatenate([weight[:share], weight[share:]], axis=1)
    other = send_team(weight, 1)
    low = lax.axis_index("team") % 2 == 0
    return total, jnp.where(low, join(weight, other), join(other, weight))


def per_device(features, weight, tiles, tile_rows, tile_cols, tile_count, cotangent):
    node_dev, fin = features.shape
    tile = tiles.shape[-1]
    slots = tiles.shape[2]
    sections = lax.axis_size("section")
    teams = lax.axis_size("team")
    row_tiles = node_dev // tile * teams
    scale = 1.0 / math.sqrt(node_dev * sections * teams)
    slab = tiles.reshape(slots, tile, tile)
    keys = slot_keys(
        tile_rows.reshape(slots),
        tile_cols.reshape(slots),
        tile_count.reshape(()),
        lax.axis_index("section"),
    )
    member = lax.axis_index("team").astype(jnp.int32).reshape(1)


    def near_call(info, pieces):
        return forward_call(0, info, member, slab, pieces, spans_of(pieces), None, row_tiles)[0]

    near_sum, far, cots, slot_info = gather_features(
        features, cotangent, keys, row_tiles, tile, near_call
    )
    mine, theirs = forward_call(
        1, slot_info, member, slab, far, spans_of(far), near_sum, row_tiles
    )
    pair = add(mine, send_team(theirs, 1)).astype(BF16)
    mine = add(pair, send_team(pair, 2)).astype(BF16)
    size = far[0].shape[0]
    output, rider, backs, *far_terms = backward_far_call(
        slot_info, member, slab, mine, send_team(mine, 1), cots, weight, size
    )
    near_terms = backward_near_call(slot_info, slab, backs, size)
    total, weight_sum = scatter_sums(near_terms, far_terms, rider)
    grad_features = total.transpose(0, 2, 1).reshape(node_dev, fin).astype(BF16)
    return output, grad_features, weight_sum * scale


def solution(mesh):
    in_specs = (
        P(("section", "team"), None),
        P(),
        P("section", "team", None, None, None),
        P("section", "team", None),
        P("section", "team", None),
        P("section", "team"),
        P(("section", "team"), None),
    )
    out_specs = (P(("section", "team"), None), P(("section", "team"), None), P())
    return jax.shard_map(
        per_device, mesh=mesh, in_specs=in_specs, out_specs=out_specs, check_vma=False
    )
```
